32 devices in a mesh: ka: 16 (over z, y, core), pa: 2 (over x).
Axes of the slice: x: 2, y: 2, z: 4, core: 2. Of those that a mesh axis runs over, the one named last changes fastest.
Arguments:
- previous: float32 [128, 256, 256], P('ka', None, 'pa'), may hold values from -6 to 6
- current: float32 [128, 256, 256], P('ka', None, 'pa'), may hold values from -6 to 6
- energies: float32 [128, 256, 256], P('ka', None, 'pa'), may hold values from -0.5 to 0.5
- valence: float32 [128, 256, 256], P('ka'), may hold values from -0.375 to 0.375
- conduction: float32 [128, 256, 256], P('ka', None, 'pa'), may hold values from -0.375 to 0.375
- kernel: float32 [128, 256, 256], P(None, 'ka', 'pa'), may hold values from 0.05 to 0.35
Outputs:
- next_one: float32 [128, 256, 256], P('ka', None, 'pa')
- next_two: float32 [128, 256, 256], P('ka', None, 'pa')
The draws below stay inside these ranges and needn't reach their ends.
All inputs are finite; a program needn't handle non-finite values.
Results may differ from the reference program's by a relative error of at most 0.000096.
Values sent between devices are 32-bit elements; how exact they have to be, the bound alone decides.
A program may use at most 64 MiB of HBM per device.

```python
import math
import jax
import jax.numpy as jnp
from jax import lax

V = 256
C = 256
P_SIZE = 256
KY = 16
NK = 128


def block_levels(stream_key, dims, shards, low, largest):
    loudness = 1.0
    for dim, parts in shards:
        steps = jax.random.uniform(jax.random.fold_in(jax.random.fold_in(stream_key, 6), dim), (parts,), jnp.float32, low / len(shards), largest / len(shards))
        loudness = loudness * jnp.repeat(jnp.exp(steps), dims[dim] // parts).reshape((-1,) + (1,) * (len(dims) - 1 - dim))
    return loudness


def scatter_about(stream_key, dims, deviation, reach, split=(), dtype=jnp.bfloat16):
    array = deviation * jax.random.normal(stream_key, dims, jnp.float32)
    if split:
        array = array * block_levels(stream_key, dims, split, -0.22, 0.18)
    return jnp.clip(array, -reach, reach).astype(dtype)


def setup_inputs(seed: int = 0) -> dict:
    arg_keys = jax.random.split(jax.random.key(seed), 7)
    previous = scatter_about(arg_keys[0], (NK, V, C), 1.0, 6.0, ((0, 16), (2, 2)), jnp.float32)
    current = scatter_about(arg_keys[1], (NK, V, C), 1.0, 6.0, ((0, 16), (2, 2)), jnp.float32)
    energies = jnp.clip(jax.random.uniform(arg_keys[2], (NK, V, C), jnp.float32, -0.5, 0.5) * block_levels(arg_keys[2], (NK, V, C), ((0, 16), (2, 2)), -0.4, 0.0), -0.5, 0.5)
    valence = scatter_about(arg_keys[3], (NK, V, P_SIZE), V ** -0.5, 0.375, ((0, 16),), jnp.float32)
    conduction = scatter_about(arg_keys[4], (NK, C, P_SIZE), C ** -0.5, 0.375, ((0, 16), (2, 2)), jnp.float32)
    kernel = jnp.clip(0.05 + 0.29999999 * jax.random.uniform(arg_keys[5], (NK, P_SIZE, P_SIZE), jnp.float32) ** block_levels(arg_keys[5], (NK, P_SIZE, P_SIZE), ((1, 16), (2, 2)), -0.2, 0.2), 0.05, 0.35)
    return {"previous": previous, "current": current, "energies": energies, "valence": valence, "conduction": conduction, "kernel": kernel}


def phase_tables(total):
    points = jnp.arange(total)
    wide = total // KY
    coarse = points // KY
    finer = points % KY
    turns = ((coarse[:, None] * coarse[None, :]) % wide).astype(jnp.float32) / wide
    turns = turns + ((finer[:, None] * finer[None, :]) % KY).astype(jnp.float32) / KY
    angles = 2.0 * math.pi * turns
    return jnp.cos(angles), jnp.sin(angles)


def kernel_product(field, valence, conduction, kernel, cosine_table, sine_table):
    total = field.shape[0]
    width = valence.shape[2]
    highest = lax.Precision.HIGHEST
    inner = jnp.einsum("kvc,kcn->kvn", field, conduction, precision=highest)
    pair_blocks = jnp.einsum("kvm,kvn->kmn", valence, inner, precision=highest)
    flattened = pair_blocks.reshape(total, width * width)
    even = jnp.dot(cosine_table, flattened, precision=highest)
    odd = jnp.dot(sine_table, flattened, precision=highest)
    weights = kernel.reshape(total, width * width)
    screened = (jnp.dot(cosine_table, weights * even, precision=highest) + jnp.dot(sine_table, weights * odd, precision=highest)) / total
    screened = screened.reshape(total, width, width)
    partial_rows = jnp.einsum("kmn,kcn->kmc", screened, conduction, precision=highest)
    return jnp.einsum("kvm,kmc->kvc", valence, partial_rows, precision=highest)


def reference(previous, current, energies, valence, conduction, kernel):
    cosine_table, sine_table = phase_tables(current.shape[0])
    first = energies * current + kernel_product(current, valence, conduction, kernel, cosine_table, sine_table)
    next_one = 2.0 * first - previous
    second = energies * next_one + kernel_product(next_one, valence, conduction, kernel, cosine_table, sine_table)
    next_two = 2.0 * second - current
    return next_one, next_two
```

```python
import functools
import math

import jax
import jax.numpy as jnp
from jax import lax
from jax.experimental import pallas as pl
from jax.experimental.pallas import tpu as pltpu
from jax.sharding import PartitionSpec as P

KY = 16
MESH = pl.DeviceIdType.MESH
LAG_NEXT = 1
LAG_PAIRS = 2


def plus(a, b, sign=1.0):
    re = a[0] + b[0] if sign > 0 else a[0] - b[0]
    if b[1] is None:
        return (re, a[1])
    if a[1] is None:
        return (re, b[1] if sign > 0 else -b[1])
    return (re, a[1] + b[1] if sign > 0 else a[1] - b[1])


def conj(a):
    return a if a[1] is None else (a[0], -a[1])


def turn(a, step, size, sign):
    eighth = 8 * step // size if 8 * step % size == 0 else None
    if eighth == 0:
        return a
    if eighth == 2:
        re = None if a[1] is None else (-a[1] if sign > 0 else a[1])
        im = a[0] if sign > 0 else -a[0]
        return (jnp.zeros_like(im) if re is None else re, im)
    c = math.cos(2.0 * math.pi * step / size)
    s = sign * math.sin(2.0 * math.pi * step / size)
    if a[1] is None:
        return (c * a[0], s * a[0])
    if eighth == 1:
        return (c * (a[0] - sign * a[1]), c * (a[1] + sign * a[0]))
    if eighth == 3:
        return (c * (a[0] + sign * a[1]), c * (a[1] - sign * a[0]))
    return (c * a[0] - s * a[1], c * a[1] + s * a[0])


def complex_transform(x, sign):
    size = len(x)
    if size == 1:
        return x
    even = complex_transform(x[0::2], sign)
    odd = complex_transform(x[1::2], sign)
    odd = [turn(o, j, size, sign) for j, o in enumerate(odd)]
    first = [plus(e, o) for e, o in zip(even, odd)]
    return first + [plus(e, o, -1.0) for e, o in zip(even, odd)]


def real_forward(x):
    size = len(x)
    if size == 1:
        return [(x[0], None)]
    even, odd = real_forward(x[0::2]), real_forward(x[1::2])
    if size == 2:
        return [plus(even[0], odd[0]), plus(even[0], odd[0], -1.0)]
    out = [None] * (size // 2 + 1)
    for j in range(size // 4):
        t = turn(odd[j], j, size, -1)
        out[j] = plus(even[j], t)
        out[size // 2 - j] = conj(plus(even[j], t, -1.0))
    out[size // 4] = (even[size // 4][0], -odd[size // 4][0])
    return out


def real_backward(spectrum):
    size = 2 * (len(spectrum) - 1)
    if size == 2:
        a, b = spectrum[0][0], spectrum[1][0]
        return [a + b, a - b]
    even, odd = [], []
    for j in range(size // 4):
        mirrored = conj(spectrum[size // 2 - j])
        even.append(plus(spectrum[j], mirrored))
        odd.append(turn(plus(spectrum[j], mirrored, -1.0), j, size, 1))
    middle = spectrum[size // 4]
    even.append((2.0 * middle[0], None))
    odd.append((-2.0 * middle[1], None))
    out = [None] * size
    out[0::2] = real_backward(even)
    out[1::2] = real_backward(odd)
    return out


def screen_in_place(ref, weights):
    total, rows = ref.shape[0], ref.shape[1]
    wide = total // KY
    half = KY // 2
    scale = 0.5 / total
    assert rows % 8 == 0

    def fine_forward(i, carry):
        base, at = (i % wide) * KY, pl.ds(pl.multiple_of((i // wide) * 8, 8), 8)
        out = real_forward([ref[base + j, at, :] for j in range(KY)])
        for j in range(half + 1):
            ref[base + j, at, :] = out[j][0]
            if 0 < j < half:
                ref[base + KY - j, at, :] = out[j][1]
        return carry

    def fine_backward(i, carry):
        base, at = (i % wide) * KY, pl.ds(pl.multiple_of((i // wide) * 8, 8), 8)
        values = [ref[base + j, at, :] for j in range(KY)]
        spectrum = [(values[0], None)]
        spectrum += [(values[j], values[KY - j]) for j in range(1, half)]
        spectrum += [(values[half], None)]
        for j, value in enumerate(real_backward(spectrum)):
            ref[base + j, at, :] = value
        return carry

    def weight(q, finer, mirror, at):
        a = weights[q * KY + finer, at, :]
        b = weights[((wide - q) % wide) * KY + mirror, at, :]
        return (a + b) * scale

    def coarse_real(i, carry):
        at = pl.ds(pl.multiple_of(i * 8, 8), 8)
        for finer in (0, half):
            out = real_forward([ref[j * KY + finer, at, :] for j in range(wide)])
            scaled = []
            for q, (re, im) in enumerate(out):
                w = weight(q, finer, finer, at)
                scaled.append((re * w, None if im is None else im * w))
            for j, value in enumerate(real_backward(scaled)):
                ref[j * KY + finer, at, :] = value
        return carry

    def coarse_complex(i, carry):
        finer = 1 + i % (half - 1)
        mirror = KY - finer
        at = pl.ds(pl.multiple_of((i // (half - 1)) * 8, 8), 8)
        x = [(ref[j * KY + finer, at, :], ref[j * KY + mirror, at, :]) for j in range(wide)]
        scaled = []
        for q, (re, im) in enumerate(complex_transform(x, -1)):
            w = weight(q, finer, mirror, at)
            scaled.append((re * w, im * w))
        for j, (re, im) in enumerate(complex_transform(scaled, 1)):
            ref[j * KY + finer, at, :] = re
            ref[j * KY + mirror, at, :] = im
        return carry

    blocks = rows // 8
    lax.fori_loop(0, blocks * wide, fine_forward, 0)
    lax.fori_loop(0, blocks, coarse_real, 0)
    lax.fori_loop(0, blocks * (half - 1), coarse_complex, 0)
    lax.fori_loop(0, blocks * wide, fine_backward, 0)


def split(a):
    high = a.astype(jnp.bfloat16)
    return high, (a - high.astype(jnp.float32)).astype(jnp.bfloat16)


def product(a, b, left, right):
    dot = functools.partial(
        lax.dot_general,
        dimension_numbers=(((left,), (right,)), ((), ())),
        preferred_element_type=jnp.float32,
    )
    (ah, al), (bh, bl) = split(a), split(b)
    return dot(ah, bh) + (dot(ah, bl) + dot(al, bh))


def fused_kernel(
    ka, previous, current, energies, valence, conduction, weights, next_one, next_two,
    other_x, pairs, owned, returned, sent_sum, other_sum, own_sum,
    x_send, x_recv, pair_send, pair_recv, back_send, back_recv, sum_send, sum_recv,
):
    me, mine = lax.axis_index("ka"), lax.axis_index("pa")
    other = 1 - mine
    count, _, width = current.shape
    rows = weights.shape[1]
    own_c = pl.ds(pl.multiple_of(mine * width, width), width)
    other_c = pl.ds(pl.multiple_of(other * width, width), width)
    own_rows = pl.ds(pl.multiple_of(me * rows, rows), rows)

    barrier = pltpu.get_barrier_semaphore()

    def greet(j, carry):
        pl.semaphore_signal(
            barrier, inc=1, device_id={"ka": lax.rem(me + j, ka)}, device_id_type=MESH
        )
        return carry

    lax.fori_loop(1, ka, greet, 0)
    pl.semaphore_signal(barrier, inc=1, device_id={"pa": other}, device_id_type=MESH)
    pl.semaphore_wait(barrier, ka)

    def x_copy(turn_, k):
        source = (current, next_one)[turn_]
        return pltpu.make_async_remote_copy(
            src_ref=source.at[k], dst_ref=other_x.at[turn_, k],
            send_sem=x_send.at[turn_, k], recv_sem=x_recv.at[turn_, k],
            device_id={"pa": other}, device_id_type=MESH,
        )

    def sum_copy(turn_, k):
        return pltpu.make_async_remote_copy(
            src_ref=sent_sum.at[turn_, k], dst_ref=other_sum.at[turn_, k],
            send_sem=sum_send.at[turn_, k], recv_sem=sum_recv.at[turn_, k],
            device_id={"pa": other}, device_id_type=MESH,
        )

    def both_halves(k):
        return jnp.concatenate([conduction[k, own_c, :], conduction[k, other_c, :]], axis=0)

    def pair_step(turn_, k):
        source = (current, next_one)[turn_]
        x_copy(turn_, k).wait_recv()
        x = jnp.concatenate([source[k], other_x[turn_, k]], axis=1)
        inner = product(x, both_halves(k), 1, 0)
        pairs[turn_, k] = product(valence[k], inner, 0, 0)

        def send(j, carry):
            peer = lax.rem(me + j, ka)
            pltpu.make_async_remote_copy(
                src_ref=pairs.at[turn_, k, pl.ds(pl.multiple_of(peer * rows, rows), rows)],
                dst_ref=owned.at[turn_, me * count + k],
                send_sem=pair_send.at[turn_], recv_sem=pair_recv.at[turn_],
                device_id={"ka": peer}, device_id_type=MESH,
            ).start()
            return carry

        lax.fori_loop(1, ka, send, 0)
        owned[turn_, me * count + k] = pairs[turn_, k, own_rows, :]

    def wait_bytes(ref, sem):
        pltpu.make_async_copy(ref, ref, sem).wait()

    def screen(turn_):
        wait_bytes(owned.at[turn_, pl.ds(0, (ka - 1) * count)], pair_recv.at[turn_])
        screen_in_place(owned.at[turn_], weights)

        def send(i, carry):
            k, j = i // (ka - 1), 1 + i % (ka - 1)
            peer = lax.rem(me + j, ka)
            pltpu.make_async_remote_copy(
                src_ref=owned.at[turn_, peer * count + k],
                dst_ref=returned.at[turn_, k, own_rows],
                send_sem=back_send.at[turn_], recv_sem=back_recv.at[turn_, k],
                device_id={"ka": peer}, device_id_type=MESH,
            ).start()
            return carry

        lax.fori_loop(0, count * (ka - 1), send, 0)

        def keep(k, carry):
            returned[turn_, k, own_rows, :] = owned[turn_, me * count + k]
            return carry

        lax.fori_loop(0, count, keep, 0)

    def sum_step(turn_, k):
        wait_bytes(returned.at[turn_, k, pl.ds(0, (ka - 1) * rows)], back_recv.at[turn_, k])
        partial_rows = product(returned[turn_, k], both_halves(k), 1, 1)
        term = product(valence[k], partial_rows, 1, 0)
        sent_sum[turn_, k] = term[:, width:]
        sum_copy(turn_, k).start()
        own_sum[k] = term[:, :width]

    def next_step(turn_, k):
        sum_copy(turn_, k).wait_recv()
        summed = own_sum[k] + other_sum[turn_, k]
        if turn_ == 0:
            next_one[k] = 2.0 * (energies[k] * current[k] + summed) - previous[k]
            x_copy(1, k).start()
        else:
            next_two[k] = 2.0 * (energies[k] * next_one[k] + summed) - current[k]

    def start_x(k, carry):
        x_copy(0, k).start()
        return carry

    lax.fori_loop(0, count, start_x, 0)

    def first_pairs(k, carry):
        pair_step(0, k)
        return carry

    lax.fori_loop(0, count, first_pairs, 0)
    screen(0)

    def middle(t, carry):
        @pl.when(t < count)
        def _():
            sum_step(0, t)

        @pl.when(jnp.logical_and(t >= LAG_NEXT, t < count + LAG_NEXT))
        def _():
            next_step(0, t - LAG_NEXT)

        @pl.when(t >= LAG_PAIRS)
        def _():
            pair_step(1, t - LAG_PAIRS)

        return carry

    lax.fori_loop(0, count + LAG_PAIRS, middle, 0)
    screen(1)

    def last(t, carry):
        @pl.when(t < count)
        def _():
            sum_step(1, t)

        @pl.when(t >= LAG_NEXT)
        def _():
            next_step(1, t - LAG_NEXT)

        return carry

    lax.fori_loop(0, count + LAG_NEXT, last, 0)

    for turn_ in (0, 1):
        def sent(k, carry):
            x_copy(turn_, k).wait_send()
            sum_copy(turn_, k).wait_send()
            return carry

        lax.fori_loop(0, count, sent, 0)
        everything = owned.at[turn_, pl.ds(0, (ka - 1) * count)]
        wait_bytes(everything, pair_send.at[turn_])
        wait_bytes(everything, back_send.at[turn_])


def fused(ka, previous, current, energies, valence, conduction, kernel):
    block, owned = current.shape, kernel.shape
    whole = pl.BlockSpec(memory_space=pltpu.VMEM)
    points = (block[0], valence.shape[2], kernel.shape[2])
    twice = lambda shape: pltpu.VMEM((2,) + shape, jnp.float32)
    dma = pltpu.SemaphoreType.DMA
    return pl.pallas_call(
        functools.partial(fused_kernel, ka),
        out_shape=(jax.ShapeDtypeStruct(block, jnp.float32),) * 2,
        in_specs=[whole] * 6,
        out_specs=(whole, whole),
        scratch_shapes=[
            twice(block), twice(points), twice(owned), twice(points),
            twice(block), twice(block), pltpu.VMEM(block, jnp.float32),
            dma((2, block[0])), dma((2, block[0])), dma((2,)), dma((2,)),
            dma((2,)), dma((2, block[0])), dma((2, block[0])), dma((2, block[0])),
        ],
        compiler_params=pltpu.CompilerParams(
            collective_id=0, has_side_effects=True, vmem_limit_bytes=52 * 2**20
        ),
    )(previous, current, energies, valence, conduction, kernel)


def phase_tables(total):
    points = jnp.arange(total)
    wide = total // KY
    coarse = points // KY
    finer = points % KY
    turns = (coarse[:, None] * coarse[None, :] % wide).astype(jnp.float32) / wide
    turns = turns + (finer[:, None] * finer[None, :] % KY).astype(jnp.float32) / KY
    angles = 2.0 * math.pi * turns
    return (jnp.cos(angles), jnp.sin(angles))


def screen_owned(flattened, kernel, cosine_table, sine_table):
    highest = lax.Precision.HIGHEST
    total = kernel.shape[0]
    even = jnp.dot(cosine_table, flattened, precision=highest)
    odd = jnp.dot(sine_table, flattened, precision=highest)
    weights = kernel.reshape(total, kernel.shape[1] * kernel.shape[2])
    return (
        jnp.dot(cosine_table, weights * even, precision=highest)
        + jnp.dot(sine_table, weights * odd, precision=highest)
    ) / total


def kernel_product(field, valence, conduction, kernel, cosine_table, sine_table):
    highest = lax.Precision.HIGHEST
    total = kernel.shape[0]
    inner = jnp.einsum("kvc,kcn->kvn", field, conduction, precision=highest)
    pair_blocks = jnp.einsum("kvm,kvn->kmn", valence, inner, precision=highest)
    owned = lax.all_to_all(pair_blocks, "ka", split_axis=1, concat_axis=0, tiled=True)
    flattened = owned.reshape(total, owned.shape[1] * owned.shape[2])
    screened = screen_owned(flattened, kernel, cosine_table, sine_table).reshape(owned.shape)
    returned = lax.all_to_all(screened, "ka", split_axis=0, concat_axis=1, tiled=True)
    partial_rows = jnp.einsum("kmn,kcn->kmc", returned, conduction, precision=highest)
    return jnp.einsum("kvm,kmc->kvc", valence, partial_rows, precision=highest)


def fits(ka, pa, current, conduction, kernel):
    wide = kernel.shape[0] // KY
    return (
        pa == 2
        and current.shape[2] == kernel.shape[2]
        and current.shape[2] % 128 == 0
        and kernel.shape[1] % 8 == 0
        and wide >= 2
        and wide & (wide - 1) == 0
    )


def on_device(ka, pa, previous, current, energies, valence, conduction, kernel):
    if fits(ka, pa, current, conduction, kernel):
        return fused(ka, previous, current, energies, valence, conduction, kernel)
    cosine_table, sine_table = phase_tables(kernel.shape[0])
    whole_current = lax.all_gather(current, "pa", axis=2, tiled=True)
    folded_term = kernel_product(
        whole_current, valence, conduction, kernel, cosine_table, sine_table
    )
    summed = lax.psum_scatter(folded_term, "pa", scatter_dimension=2, tiled=True)
    next_one = 2.0 * (energies * current + summed) - previous
    whole_next = lax.all_gather(next_one, "pa", axis=2, tiled=True)
    second_term = kernel_product(whole_next, valence, conduction, kernel, cosine_table, sine_table)
    second_sum = lax.psum_scatter(second_term, "pa", scatter_dimension=2, tiled=True)
    next_two = 2.0 * (energies * next_one + second_sum) - current
    return (next_one, next_two)


def solution(mesh):
    placed = (
        P("ka", None, "pa"),
        P("ka", None, "pa"),
        P("ka", None, "pa"),
        P("ka", None, None),
        P("ka", None, "pa"),
        P(None, "ka", "pa"),
    )
    return jax.shard_map(
        functools.partial(on_device, mesh.shape["ka"], mesh.shape["pa"]),
        mesh=mesh,
        in_specs=placed,
        out_specs=(P("ka", None, "pa"), P("ka", None, "pa")),
        check_vma=False,
    )
```

```python
import functools
import math

import jax
import jax.numpy as jnp
from jax import lax
from jax.experimental import pallas as pl
from jax.experimental.pallas import tpu as pltpu
from jax.sharding import PartitionSpec as P

KY = 16
MESH = pl.DeviceIdType.MESH
LAG_NEXT = 2
LAG_PAIRS = 4
AHEAD = 3


def plus(a, b, sign=1.0):
    re = a[0] + b[0] if sign > 0 else a[0] - b[0]
    if b[1] is None:
        return (re, a[1])
    if a[1] is None:
        return (re, b[1] if sign > 0 else -b[1])
    return (re, a[1] + b[1] if sign > 0 else a[1] - b[1])


def conj(a):
    return a if a[1] is None else (a[0], -a[1])


def turn(a, step, size, sign):
    eighth = 8 * step // size if 8 * step % size == 0 else None
    if eighth == 0:
        return a
    if eighth == 2:
        re = None if a[1] is None else (-a[1] if sign > 0 else a[1])
        im = a[0] if sign > 0 else -a[0]
        return (jnp.zeros_like(im) if re is None else re, im)
    c = math.cos(2.0 * math.pi * step / size)
    s = sign * math.sin(2.0 * math.pi * step / size)
    if a[1] is None:
        return (c * a[0], s * a[0])
    if eighth == 1:
        return (c * (a[0] - sign * a[1]), c * (a[1] + sign * a[0]))
    if eighth == 3:
        return (c * (a[0] + sign * a[1]), c * (a[1] - sign * a[0]))
    return (c * a[0] - s * a[1], c * a[1] + s * a[0])


def complex_transform(x, sign):
    size = len(x)
    if size == 1:
        return x
    even = complex_transform(x[0::2], sign)
    odd = complex_transform(x[1::2], sign)
    odd = [turn(o, j, size, sign) for j, o in enumerate(odd)]
    first = [plus(e, o) for e, o in zip(even, odd)]
    return first + [plus(e, o, -1.0) for e, o in zip(even, odd)]


def real_forward(x):
    size = len(x)
    if size == 1:
        return [(x[0], None)]
    even, odd = real_forward(x[0::2]), real_forward(x[1::2])
    if size == 2:
        return [plus(even[0], odd[0]), plus(even[0], odd[0], -1.0)]
    out = [None] * (size // 2 + 1)
    for j in range(size // 4):
        t = turn(odd[j], j, size, -1)
        out[j] = plus(even[j], t)
        out[size // 2 - j] = conj(plus(even[j], t, -1.0))
    out[size // 4] = (even[size // 4][0], -odd[size // 4][0])
    return out


def real_backward(spectrum):
    size = 2 * (len(spectrum) - 1)
    if size == 2:
        a, b = spectrum[0][0], spectrum[1][0]
        return [a + b, a - b]
    even, odd = [], []
    for j in range(size // 4):
        mirrored = conj(spectrum[size // 2 - j])
        even.append(plus(spectrum[j], mirrored))
        odd.append(turn(plus(spectrum[j], mirrored, -1.0), j, size, 1))
    middle = spectrum[size // 4]
    even.append((2.0 * middle[0], None))
    odd.append((-2.0 * middle[1], None))
    out = [None] * size
    out[0::2] = real_backward(even)
    out[1::2] = real_backward(odd)
    return out


def screen_in_place(ref, weights):
    total, rows = ref.shape[0], ref.shape[1]
    wide = total // KY
    half = KY // 2
    scale = 0.5 / total
    assert rows % 8 == 0

    def fine_forward(i, carry):
        base, at = (i % wide) * KY, pl.ds(pl.multiple_of((i // wide) * 8, 8), 8)
        out = real_forward([ref[base + j, at, :] for j in range(KY)])
        for j in range(half + 1):
            ref[base + j, at, :] = out[j][0]
            if 0 < j < half:
                ref[base + KY - j, at, :] = out[j][1]
        return carry

    def fine_backward(i, carry):
        base, at = (i % wide) * KY, pl.ds(pl.multiple_of((i // wide) * 8, 8), 8)
        values = [ref[base + j, at, :] for j in range(KY)]
        spectrum = [(values[0], None)]
        spectrum += [(values[j], values[KY - j]) for j in range(1, half)]
        spectrum += [(values[half], None)]
        for j, value in enumerate(real_backward(spectrum)):
            ref[base + j, at, :] = value
        return carry

    def weight(q, finer, mirror, at):
        a = weights[q * KY + finer, at, :]
        b = weights[((wide - q) % wide) * KY + mirror, at, :]
        return (a + b) * scale

    def coarse_real(i, carry):
        at = pl.ds(pl.multiple_of(i * 8, 8), 8)
        for finer in (0, half):
            out = real_forward([ref[j * KY + finer, at, :] for j in range(wide)])
            scaled = []
            for q, (re, im) in enumerate(out):
                w = weight(q, finer, finer, at)
                scaled.append((re * w, None if im is None else im * w))
            for j, value in enumerate(real_backward(scaled)):
                ref[j * KY + finer, at, :] = value
        return carry

    def coarse_complex(i, carry):
        finer = 1 + i % (half - 1)
        mirror = KY - finer
        at = pl.ds(pl.multiple_of((i // (half - 1)) * 8, 8), 8)
        x = [(ref[j * KY + finer, at, :], ref[j * KY + mirror, at, :]) for j in range(wide)]
        scaled = []
        for q, (re, im) in enumerate(complex_transform(x, -1)):
            w = weight(q, finer, mirror, at)
            scaled.append((re * w, im * w))
        for j, (re, im) in enumerate(complex_transform(scaled, 1)):
            ref[j * KY + finer, at, :] = re
            ref[j * KY + mirror, at, :] = im
        return carry

    blocks = rows // 8
    lax.fori_loop(0, blocks * wide, fine_forward, 0)
    lax.fori_loop(0, blocks, coarse_real, 0)
    lax.fori_loop(0, blocks * (half - 1), coarse_complex, 0)
    lax.fori_loop(0, blocks * wide, fine_backward, 0)


def split(a):
    high = a.astype(jnp.bfloat16)
    return high, (a - high.astype(jnp.float32)).astype(jnp.bfloat16)


def product(a, b, left, right):
    dot = functools.partial(
        lax.dot_general,
        dimension_numbers=(((left,), (right,)), ((), ())),
        preferred_element_type=jnp.float32,
    )
    (ah, al), (bh, bl) = split(a), split(b)
    return dot(ah, bh) + (dot(ah, bl) + dot(al, bh))


def fused_kernel(
    ka, previous, current, energies, valence, conduction, weights, next_one, next_two,
    other_x, pairs, owned, returned, sent_sum, other_sum, own_sum,
    x_send, x_recv, pair_send, pair_recv, back_send, back_recv, sum_send, sum_recv,
):
    me, mine = lax.axis_index("ka"), lax.axis_index("pa")
    other = 1 - mine
    count, _, width = current.shape
    rows = weights.shape[1]
    own_c = pl.ds(pl.multiple_of(mine * width, width), width)
    other_c = pl.ds(pl.multiple_of(other * width, width), width)
    own_rows = pl.ds(pl.multiple_of(me * rows, rows), rows)

    barrier = pltpu.get_barrier_semaphore()

    def greet(j, carry):
        pl.semaphore_signal(
            barrier, inc=1, device_id={"ka": lax.rem(me + j, ka)}, device_id_type=MESH
        )
        return carry

    lax.fori_loop(1, ka, greet, 0)
    pl.semaphore_signal(barrier, inc=1, device_id={"pa": other}, device_id_type=MESH)
    pl.semaphore_wait(barrier, ka)

    def x_copy(turn_, k):
        source = (current, next_one)[turn_]
        return pltpu.make_async_remote_copy(
            src_ref=source.at[k], dst_ref=other_x.at[turn_, k],
            send_sem=x_send.at[turn_, k], recv_sem=x_recv.at[turn_, k],
            device_id={"pa": other}, device_id_type=MESH,
        )

    def sum_copy(turn_, k):
        return pltpu.make_async_remote_copy(
            src_ref=sent_sum.at[turn_, k], dst_ref=other_sum.at[turn_, k],
            send_sem=sum_send.at[turn_, k], recv_sem=sum_recv.at[turn_, k],
            device_id={"pa": other}, device_id_type=MESH,
        )

    def both_halves(k):
        return jnp.concatenate([conduction[k, own_c, :], conduction[k, other_c, :]], axis=0)

    def pair_step(turn_, k):
        source = (current, next_one)[turn_]
        x_copy(turn_, k).wait_recv()
        if turn_ == 0:
            @pl.when(k + AHEAD < count)
            def _():
                x_copy(0, k + AHEAD).start()
        x = jnp.concatenate([source[k], other_x[turn_, k]], axis=1)
        inner = product(x, both_halves(k), 1, 0)
        pairs[turn_, k] = product(valence[k], inner, 0, 0)

        def send(j, carry):
            peer = lax.rem(me + j, ka)
            pltpu.make_async_remote_copy(
                src_ref=pairs.at[turn_, k, pl.ds(pl.multiple_of(peer * rows, rows), rows)],
                dst_ref=owned.at[turn_, me * count + k],
                send_sem=pair_send.at[turn_], recv_sem=pair_recv.at[turn_],
                device_id={"ka": peer}, device_id_type=MESH,
            ).start()
            return carry

        lax.fori_loop(1, ka, send, 0)
        owned[turn_, me * count + k] = pairs[turn_, k, own_rows, :]

    def wait_bytes(ref, sem):
        pltpu.make_async_copy(ref, ref, sem).wait()

    def send_back(turn_, k):
        def send(j, carry):
            peer = lax.rem(me + j, ka)
            pltpu.make_async_remote_copy(
                src_ref=owned.at[turn_, peer * count + k],
                dst_ref=returned.at[turn_, k, own_rows],
                send_sem=back_send.at[turn_], recv_sem=back_recv.at[turn_, k],
                device_id={"ka": peer}, device_id_type=MESH,
            ).start()
            return carry

        lax.fori_loop(1, ka, send, 0)

    def screen(turn_):
        wait_bytes(owned.at[turn_, pl.ds(0, (ka - 1) * count)], pair_recv.at[turn_])
        screen_in_place(owned.at[turn_], weights)

        for k in range(min(AHEAD, count)):
            send_back(turn_, k)

        def keep(k, carry):
            returned[turn_, k, own_rows, :] = owned[turn_, me * count + k]
            return carry

        lax.fori_loop(0, count, keep, 0)

    def sum_step(turn_, k):
        wait_bytes(returned.at[turn_, k, pl.ds(0, (ka - 1) * rows)], back_recv.at[turn_, k])

        @pl.when(k + AHEAD < count)
        def _():
            send_back(turn_, k + AHEAD)

        partial_rows = product(returned[turn_, k], both_halves(k), 1, 1)
        term = product(valence[k], partial_rows, 1, 0)
        sent_sum[turn_, k] = term[:, width:]
        sum_copy(turn_, k).start()
        own_sum[k] = term[:, :width]

    def next_step(turn_, k):
        sum_copy(turn_, k).wait_recv()
        summed = own_sum[k] + other_sum[turn_, k]
        if turn_ == 0:
            next_one[k] = 2.0 * (energies[k] * current[k] + summed) - previous[k]
            x_copy(1, k).start()
        else:
            next_two[k] = 2.0 * (energies[k] * next_one[k] + summed) - current[k]

    def start_x(k, carry):
        x_copy(0, k).start()
        return carry

    lax.fori_loop(0, min(AHEAD, count), start_x, 0)

    def first_pairs(k, carry):
        pair_step(0, k)
        return carry

    lax.fori_loop(0, count, first_pairs, 0)
    screen(0)

    def middle(t, carry):
        @pl.when(t < count)
        def _():
            sum_step(0, t)

        @pl.when(jnp.logical_and(t >= LAG_NEXT, t < count + LAG_NEXT))
        def _():
            next_step(0, t - LAG_NEXT)

        @pl.when(t >= LAG_PAIRS)
        def _():
            pair_step(1, t - LAG_PAIRS)

        return carry

    lax.fori_loop(0, count + LAG_PAIRS, middle, 0)
    screen(1)

    def last(t, carry):
        @pl.when(t < count)
        def _():
            sum_step(1, t)

        @pl.when(t >= LAG_NEXT)
        def _():
            next_step(1, t - LAG_NEXT)

        return carry

    lax.fori_loop(0, count + LAG_NEXT, last, 0)

    for turn_ in (0, 1):
        def sent(k, carry):
            x_copy(turn_, k).wait_send()
            sum_copy(turn_, k).wait_send()
            return carry

        lax.fori_loop(0, count, sent, 0)
        everything = owned.at[turn_, pl.ds(0, (ka - 1) * count)]
        wait_bytes(everything, pair_send.at[turn_])
        wait_bytes(everything, back_send.at[turn_])


def fused(ka, previous, current, energies, valence, conduction, kernel):
    block, owned = current.shape, kernel.shape
    whole = pl.BlockSpec(memory_space=pltpu.VMEM)
    points = (block[0], valence.shape[2], kernel.shape[2])
    twice = lambda shape: pltpu.VMEM((2,) + shape, jnp.float32)
    dma = pltpu.SemaphoreType.DMA
    return pl.pallas_call(
        functools.partial(fused_kernel, ka),
        out_shape=(jax.ShapeDtypeStruct(block, jnp.float32),) * 2,
        in_specs=[whole] * 6,
        out_specs=(whole, whole),
        scratch_shapes=[
            twice(block), twice(points), twice(owned), twice(points),
            twice(block), twice(block), pltpu.VMEM(block, jnp.float32),
            dma((2, block[0])), dma((2, block[0])), dma((2,)), dma((2,)),
            dma((2,)), dma((2, block[0])), dma((2, block[0])), dma((2, block[0])),
        ],
        compiler_params=pltpu.CompilerParams(
            collective_id=0, has_side_effects=True, vmem_limit_bytes=52 * 2**20
        ),
    )(previous, current, energies, valence, conduction, kernel)


def phase_tables(total):
    points = jnp.arange(total)
    wide = total // KY
    coarse = points // KY
    finer = points % KY
    turns = (coarse[:, None] * coarse[None, :] % wide).astype(jnp.float32) / wide
    turns = turns + (finer[:, None] * finer[None, :] % KY).astype(jnp.float32) / KY
    angles = 2.0 * math.pi * turns
    return (jnp.cos(angles), jnp.sin(angles))


def screen_owned(flattened, kernel, cosine_table, sine_table):
    highest = lax.Precision.HIGHEST
    total = kernel.shape[0]
    even = jnp.dot(cosine_table, flattened, precision=highest)
    odd = jnp.dot(sine_table, flattened, precision=highest)
    weights = kernel.reshape(total, kernel.shape[1] * kernel.shape[2])
    return (
        jnp.dot(cosine_table, weights * even, precision=highest)
        + jnp.dot(sine_table, weights * odd, precision=highest)
    ) / total


def kernel_product(field, valence, conduction, kernel, cosine_table, sine_table):
    highest = lax.Precision.HIGHEST
    total = kernel.shape[0]
    inner = jnp.einsum("kvc,kcn->kvn", field, conduction, precision=highest)
    pair_blocks = jnp.einsum("kvm,kvn->kmn", valence, inner, precision=highest)
    owned = lax.all_to_all(pair_blocks, "ka", split_axis=1, concat_axis=0, tiled=True)
    flattened = owned.reshape(total, owned.shape[1] * owned.shape[2])
    screened = screen_owned(flattened, kernel, cosine_table, sine_table).reshape(owned.shape)
    returned = lax.all_to_all(screened, "ka", split_axis=0, concat_axis=1, tiled=True)
    partial_rows = jnp.einsum("kmn,kcn->kmc", returned, conduction, precision=highest)
    return jnp.einsum("kvm,kmc->kvc", valence, partial_rows, precision=highest)


def fits(ka, pa, current, conduction, kernel):
    wide = kernel.shape[0] // KY
    return (
        pa == 2
        and current.shape[2] == kernel.shape[2]
        and current.shape[2] % 128 == 0
        and kernel.shape[1] % 8 == 0
        and wide >= 2
        and wide & (wide - 1) == 0
    )


def on_device(ka, pa, previous, current, energies, valence, conduction, kernel):
    if fits(ka, pa, current, conduction, kernel):
        return fused(ka, previous, current, energies, valence, conduction, kernel)
    cosine_table, sine_table = phase_tables(kernel.shape[0])
    whole_current = lax.all_gather(current, "pa", axis=2, tiled=True)
    folded_term = kernel_product(
        whole_current, valence, conduction, kernel, cosine_table, sine_table
    )
    summed = lax.psum_scatter(folded_term, "pa", scatter_dimension=2, tiled=True)
    next_one = 2.0 * (energies * current + summed) - previous
    whole_next = lax.all_gather(next_one, "pa", axis=2, tiled=True)
    second_term = kernel_product(whole_next, valence, conduction, kernel, cosine_table, sine_table)
    second_sum = lax.psum_scatter(second_term, "pa", scatter_dimension=2, tiled=True)
    next_two = 2.0 * (energies * next_one + second_sum) - current
    return (next_one, next_two)


def solution(mesh):
    placed = (
        P("ka", None, "pa"),
        P("ka", None, "pa"),
        P("ka", None, "pa"),
        P("ka", None, None),
        P("ka", None, "pa"),
        P(None, "ka", "pa"),
    )
    return jax.shard_map(
        functools.partial(on_device, mesh.shape["ka"], mesh.shape["pa"]),
        mesh=mesh,
        in_specs=placed,
        out_specs=(P("ka", None, "pa"), P("ka", None, "pa")),
        check_vma=False,
    )
```

```python
import functools
import math

import jax
import jax.numpy as jnp
from jax import lax
from jax.experimental import pallas as pl
from jax.experimental.pallas import tpu as pltpu
from jax.sharding import PartitionSpec as P

KY = 16
MESH = pl.DeviceIdType.MESH
LAG_NEXT = 2
LAG_PAIRS = 4
AHEAD = 3
GROUP = 2


def plus(a, b, sign=1.0):
    re = a[0] + b[0] if sign > 0 else a[0] - b[0]
    if b[1] is None:
        return (re, a[1])
    if a[1] is None:
        return (re, b[1] if sign > 0 else -b[1])
    return (re, a[1] + b[1] if sign > 0 else a[1] - b[1])


def conj(a):
    return a if a[1] is None else (a[0], -a[1])


def turn(a, step, size, sign):
    eighth = 8 * step // size if 8 * step % size == 0 else None
    if eighth == 0:
        return a
    if eighth == 2:
        re = None if a[1] is None else (-a[1] if sign > 0 else a[1])
        im = a[0] if sign > 0 else -a[0]
        return (jnp.zeros_like(im) if re is None else re, im)
    c = math.cos(2.0 * math.pi * step / size)
    s = sign * math.sin(2.0 * math.pi * step / size)
    if a[1] is None:
        return (c * a[0], s * a[0])
    if eighth == 1:
        return (c * (a[0] - sign * a[1]), c * (a[1] + sign * a[0]))
    if eighth == 3:
        return (c * (a[0] + sign * a[1]), c * (a[1] - sign * a[0]))
    return (c * a[0] - s * a[1], c * a[1] + s * a[0])


def complex_transform(x, sign):
    size = len(x)
    if size == 1:
        return x
    even = complex_transform(x[0::2], sign)
    odd = complex_transform(x[1::2], sign)
    odd = [turn(o, j, size, sign) for j, o in enumerate(odd)]
    first = [plus(e, o) for e, o in zip(even, odd)]
    return first + [plus(e, o, -1.0) for e, o in zip(even, odd)]


def real_forward(x):
    size = len(x)
    if size == 1:
        return [(x[0], None)]
    even, odd = real_forward(x[0::2]), real_forward(x[1::2])
    if size == 2:
        return [plus(even[0], odd[0]), plus(even[0], odd[0], -1.0)]
    out = [None] * (size // 2 + 1)
    for j in range(size // 4):
        t = turn(odd[j], j, size, -1)
        out[j] = plus(even[j], t)
        out[size // 2 - j] = conj(plus(even[j], t, -1.0))
    out[size // 4] = (even[size // 4][0], -odd[size // 4][0])
    return out


def real_backward(spectrum):
    size = 2 * (len(spectrum) - 1)
    if size == 2:
        a, b = spectrum[0][0], spectrum[1][0]
        return [a + b, a - b]
    even, odd = [], []
    for j in range(size // 4):
        mirrored = conj(spectrum[size // 2 - j])
        even.append(plus(spectrum[j], mirrored))
        odd.append(turn(plus(spectrum[j], mirrored, -1.0), j, size, 1))
    middle = spectrum[size // 4]
    even.append((2.0 * middle[0], None))
    odd.append((-2.0 * middle[1], None))
    out = [None] * size
    out[0::2] = real_backward(even)
    out[1::2] = real_backward(odd)
    return out


def screen_in_place(ref, weights):
    total, rows = ref.shape[0], ref.shape[1]
    wide = total // KY
    half = KY // 2
    scale = 0.5 / total
    assert rows % 8 == 0

    def fine_forward(i, carry):
        base, at = (i % wide) * KY, pl.ds(pl.multiple_of((i // wide) * 8, 8), 8)
        out = real_forward([ref[base + j, at, :] for j in range(KY)])
        for j in range(half + 1):
            ref[base + j, at, :] = out[j][0]
            if 0 < j < half:
                ref[base + KY - j, at, :] = out[j][1]
        return carry

    def fine_backward(i, carry):
        base, at = (i % wide) * KY, pl.ds(pl.multiple_of((i // wide) * 8, 8), 8)
        values = [ref[base + j, at, :] for j in range(KY)]
        spectrum = [(values[0], None)]
        spectrum += [(values[j], values[KY - j]) for j in range(1, half)]
        spectrum += [(values[half], None)]
        for j, value in enumerate(real_backward(spectrum)):
            ref[base + j, at, :] = value
        return carry

    def weight(q, finer, mirror, at):
        a = weights[q * KY + finer, at, :]
        b = weights[((wide - q) % wide) * KY + mirror, at, :]
        return (a + b) * scale

    def coarse_real(i, carry):
        at = pl.ds(pl.multiple_of(i * 8, 8), 8)
        for finer in (0, half):
            out = real_forward([ref[j * KY + finer, at, :] for j in range(wide)])
            scaled = []
            for q, (re, im) in enumerate(out):
                w = weight(q, finer, finer, at)
                scaled.append((re * w, None if im is None else im * w))
            for j, value in enumerate(real_backward(scaled)):
                ref[j * KY + finer, at, :] = value
        return carry

    def coarse_complex(i, carry):
        finer = 1 + i % (half - 1)
        mirror = KY - finer
        at = pl.ds(pl.multiple_of((i // (half - 1)) * 8, 8), 8)
        x = [(ref[j * KY + finer, at, :], ref[j * KY + mirror, at, :]) for j in range(wide)]
        scaled = []
        for q, (re, im) in enumerate(complex_transform(x, -1)):
            w = weight(q, finer, mirror, at)
            scaled.append((re * w, im * w))
        for j, (re, im) in enumerate(complex_transform(scaled, 1)):
            ref[j * KY + finer, at, :] = re
            ref[j * KY + mirror, at, :] = im
        return carry

    blocks = rows // 8
    lax.fori_loop(0, blocks * wide, fine_forward, 0)
    lax.fori_loop(0, blocks, coarse_real, 0)
    lax.fori_loop(0, blocks * (half - 1), coarse_complex, 0)
    lax.fori_loop(0, blocks * wide, fine_backward, 0)


def split(a):
    high = a.astype(jnp.bfloat16)
    return high, (a - high.astype(jnp.float32)).astype(jnp.bfloat16)


def product(a, b, left, right):
    (ah, al), (bh, bl) = a, b
    return lax.dot_general(
        jnp.concatenate([ah, ah, al], axis=left),
        jnp.concatenate([bh, bl, bh], axis=right),
        dimension_numbers=(((left,), (right,)), ((), ())),
        preferred_element_type=jnp.float32,
    )


def fused_kernel(
    ka, previous, current, energies, valence, conduction, weights, next_one, next_two,
    other_x, pairs, owned, returned, sent_sum, other_sum, own_sum,
    turned_parts, valence_parts, conduction_parts,
    x_send, x_recv, pair_send, pair_recv, back_send, back_recv, sum_send, sum_recv,
):
    me, mine = lax.axis_index("ka"), lax.axis_index("pa")
    other = 1 - mine
    count, _, width = current.shape
    rows = weights.shape[1]
    own_c = pl.ds(pl.multiple_of(mine * width, width), width)
    other_c = pl.ds(pl.multiple_of(other * width, width), width)
    own_rows = pl.ds(pl.multiple_of(me * rows, rows), rows)

    barrier = pltpu.get_barrier_semaphore()

    def greet(j, carry):
        pl.semaphore_signal(
            barrier, inc=1, device_id={"ka": lax.rem(me + j, ka)}, device_id_type=MESH
        )
        return carry

    lax.fori_loop(1, ka, greet, 0)
    pl.semaphore_signal(barrier, inc=1, device_id={"pa": other}, device_id_type=MESH)
    pl.semaphore_wait(barrier, ka)

    def x_copy(turn_, k):
        source = (current, next_one)[turn_]
        return pltpu.make_async_remote_copy(
            src_ref=source.at[k], dst_ref=other_x.at[turn_, k],
            send_sem=x_send.at[turn_, k], recv_sem=x_recv.at[turn_, k],
            device_id={"pa": other}, device_id_type=MESH,
        )

    def sum_copy(turn_, k):
        return pltpu.make_async_remote_copy(
            src_ref=sent_sum.at[turn_, k], dst_ref=other_sum.at[turn_, k],
            send_sem=sum_send.at[turn_, k], recv_sem=sum_recv.at[turn_, k],
            device_id={"pa": other}, device_id_type=MESH,
        )

    def prepare(k, carry):
        rows_of = jnp.concatenate([conduction[k, own_c, :], conduction[k, other_c, :]], axis=0)
        conduction_parts[0, k], conduction_parts[1, k] = split(rows_of)
        valence_parts[0, k], valence_parts[1, k] = split(valence[k])
        turned_parts[0, k], turned_parts[1, k] = split(valence[k].T)
        return carry

    def parts(ref, k):
        return ref[0, k], ref[1, k]

    def pair_step(turn_, k):
        source = (current, next_one)[turn_]
        x_copy(turn_, k).wait_recv()
        if turn_ == 0:
            @pl.when(k + AHEAD < count)
            def _():
                x_copy(0, k + AHEAD).start()
        x = jnp.concatenate([source[k], other_x[turn_, k]], axis=1)
        inner = product(split(x), parts(conduction_parts, k), 1, 0)
        pairs[turn_, k] = product(parts(turned_parts, k), split(inner), 1, 0)

        owned[turn_, me * count + k] = pairs[turn_, k, own_rows, :]

        @pl.when(k % GROUP == GROUP - 1)
        def _():
            start = k - (GROUP - 1)
            for j in range(1, ka):
                peer = lax.rem(me + j, ka)
                mark = pl.ds(pl.multiple_of(peer * rows, rows), rows)
                pltpu.make_async_remote_copy(
                    src_ref=pairs.at[turn_, pl.ds(start, GROUP), mark],
                    dst_ref=owned.at[turn_, pl.ds(me * count + start, GROUP)],
                    send_sem=pair_send.at[turn_], recv_sem=pair_recv.at[turn_],
                    device_id={"ka": peer}, device_id_type=MESH,
                ).start()

    def wait_bytes(ref, sem):
        pltpu.make_async_copy(ref, ref, sem).wait()

    def send_back(turn_, g):
        for j in range(1, ka):
            peer = lax.rem(me + j, ka)
            pltpu.make_async_remote_copy(
                src_ref=owned.at[turn_, pl.ds(peer * count + g * GROUP, GROUP)],
                dst_ref=returned.at[turn_, pl.ds(g * GROUP, GROUP), own_rows],
                send_sem=back_send.at[turn_], recv_sem=back_recv.at[turn_, g],
                device_id={"ka": peer}, device_id_type=MESH,
            ).start()

    def screen(turn_):
        wait_bytes(owned.at[turn_, pl.ds(0, (ka - 1) * count)], pair_recv.at[turn_])
        screen_in_place(owned.at[turn_], weights)

        send_back(turn_, 0)
        if count > GROUP:
            send_back(turn_, 1)

        def keep(k, carry):
            returned[turn_, k, own_rows, :] = owned[turn_, me * count + k]
            return carry

        lax.fori_loop(0, count, keep, 0)

    def sum_step(turn_, k):
        @pl.when(k % GROUP == 0)
        def _():
            g = k // GROUP
            group = pl.ds(k, GROUP)
            wait_bytes(returned.at[turn_, group, pl.ds(0, (ka - 1) * rows)], back_recv.at[turn_, g])

            @pl.when(g + 2 < count // GROUP)
            def _():
                send_back(turn_, g + 2)

        partial_rows = product(split(returned[turn_, k]), parts(conduction_parts, k), 1, 1)
        term = product(parts(valence_parts, k), split(partial_rows), 1, 0)
        sent_sum[turn_, k] = term[:, width:]
        sum_copy(turn_, k).start()
        own_sum[k] = term[:, :width]

    def next_step(turn_, k):
        sum_copy(turn_, k).wait_recv()
        summed = own_sum[k] + other_sum[turn_, k]
        if turn_ == 0:
            next_one[k] = 2.0 * (energies[k] * current[k] + summed) - previous[k]
            x_copy(1, k).start()
        else:
            next_two[k] = 2.0 * (energies[k] * next_one[k] + summed) - current[k]

    def start_x(k, carry):
        x_copy(0, k).start()
        return carry

    lax.fori_loop(0, min(AHEAD, count), start_x, 0)
    lax.fori_loop(0, count, prepare, 0)

    def first_pairs(k, carry):
        pair_step(0, k)
        return carry

    lax.fori_loop(0, count, first_pairs, 0)
    screen(0)

    def middle(t, carry):
        @pl.when(t < count)
        def _():
            sum_step(0, t)

        @pl.when(jnp.logical_and(t >= LAG_NEXT, t < count + LAG_NEXT))
        def _():
            next_step(0, t - LAG_NEXT)

        @pl.when(t >= LAG_PAIRS)
        def _():
            pair_step(1, t - LAG_PAIRS)

        return carry

    lax.fori_loop(0, count + LAG_PAIRS, middle, 0)
    screen(1)

    def last(t, carry):
        @pl.when(t < count)
        def _():
            sum_step(1, t)

        @pl.when(t >= LAG_NEXT)
        def _():
            next_step(1, t - LAG_NEXT)

        return carry

    lax.fori_loop(0, count + LAG_NEXT, last, 0)

    for turn_ in (0, 1):
        def sent(k, carry):
            x_copy(turn_, k).wait_send()
            sum_copy(turn_, k).wait_send()
            return carry

        lax.fori_loop(0, count, sent, 0)
        everything = owned.at[turn_, pl.ds(0, (ka - 1) * count)]
        wait_bytes(everything, pair_send.at[turn_])
        wait_bytes(everything, back_send.at[turn_])


def fused(ka, previous, current, energies, valence, conduction, kernel):
    block, owned = current.shape, kernel.shape
    whole = pl.BlockSpec(memory_space=pltpu.VMEM)
    points = (block[0], valence.shape[2], kernel.shape[2])
    twice = lambda shape: pltpu.VMEM((2,) + shape, jnp.float32)
    halves = lambda *shape: pltpu.VMEM((2,) + shape, jnp.bfloat16)
    dma = pltpu.SemaphoreType.DMA
    return pl.pallas_call(
        functools.partial(fused_kernel, ka),
        out_shape=(jax.ShapeDtypeStruct(block, jnp.float32),) * 2,
        in_specs=[whole] * 6,
        out_specs=(whole, whole),
        scratch_shapes=[
            twice(block), twice(points), twice(owned), twice(points),
            twice(block), twice(block), pltpu.VMEM(block, jnp.float32),
            halves(points[0], points[1], valence.shape[1]), halves(*valence.shape),
            halves(*conduction.shape),
            dma((2, block[0])), dma((2, block[0])), dma((2,)), dma((2,)),
            dma((2,)), dma((2, block[0])), dma((2, block[0])), dma((2, block[0])),
        ],
        compiler_params=pltpu.CompilerParams(
            collective_id=0, has_side_effects=True, vmem_limit_bytes=52 * 2**20
        ),
    )(previous, current, energies, valence, conduction, kernel)


def phase_tables(total):
    points = jnp.arange(total)
    wide = total // KY
    coarse = points // KY
    finer = points % KY
    turns = (coarse[:, None] * coarse[None, :] % wide).astype(jnp.float32) / wide
    turns = turns + (finer[:, None] * finer[None, :] % KY).astype(jnp.float32) / KY
    angles = 2.0 * math.pi * turns
    return (jnp.cos(angles), jnp.sin(angles))


def screen_owned(flattened, kernel, cosine_table, sine_table):
    highest = lax.Precision.HIGHEST
    total = kernel.shape[0]
    even = jnp.dot(cosine_table, flattened, precision=highest)
    odd = jnp.dot(sine_table, flattened, precision=highest)
    weights = kernel.reshape(total, kernel.shape[1] * kernel.shape[2])
    return (
        jnp.dot(cosine_table, weights * even, precision=highest)
        + jnp.dot(sine_table, weights * odd, precision=highest)
    ) / total


def kernel_product(field, valence, conduction, kernel, cosine_table, sine_table):
    highest = lax.Precision.HIGHEST
    total = kernel.shape[0]
    inner = jnp.einsum("kvc,kcn->kvn", field, conduction, precision=highest)
    pair_blocks = jnp.einsum("kvm,kvn->kmn", valence, inner, precision=highest)
    owned = lax.all_to_all(pair_blocks, "ka", split_axis=1, concat_axis=0, tiled=True)
    flattened = owned.reshape(total, owned.shape[1] * owned.shape[2])
    screened = screen_owned(flattened, kernel, cosine_table, sine_table).reshape(owned.shape)
    returned = lax.all_to_all(screened, "ka", split_axis=0, concat_axis=1, tiled=True)
    partial_rows = jnp.einsum("kmn,kcn->kmc", returned, conduction, precision=highest)
    return jnp.einsum("kvm,kmc->kvc", valence, partial_rows, precision=highest)


def fits(ka, pa, current, conduction, kernel):
    wide = kernel.shape[0] // KY
    return (
        pa == 2
        and current.shape[2] == kernel.shape[2]
        and current.shape[2] % 128 == 0
        and kernel.shape[1] % 8 == 0
        and current.shape[0] % GROUP == 0
        and wide >= 2
        and wide & (wide - 1) == 0
    )


def on_device(ka, pa, previous, current, energies, valence, conduction, kernel):
    if fits(ka, pa, current, conduction, kernel):
        return fused(ka, previous, current, energies, valence, conduction, kernel)
    cosine_table, sine_table = phase_tables(kernel.shape[0])
    whole_current = lax.all_gather(current, "pa", axis=2, tiled=True)
    folded_term = kernel_product(
        whole_current, valence, conduction, kernel, cosine_table, sine_table
    )
    summed = lax.psum_scatter(folded_term, "pa", scatter_dimension=2, tiled=True)
    next_one = 2.0 * (energies * current + summed) - previous
    whole_next = lax.all_gather(next_one, "pa", axis=2, tiled=True)
    second_term = kernel_product(whole_next, valence, conduction, kernel, cosine_table, sine_table)
    second_sum = lax.psum_scatter(second_term, "pa", scatter_dimension=2, tiled=True)
    next_two = 2.0 * (energies * next_one + second_sum) - current
    return (next_one, next_two)


def solution(mesh):
    placed = (
        P("ka", None, "pa"),
        P("ka", None, "pa"),
        P("ka", None, "pa"),
        P("ka", None, None),
        P("ka", None, "pa"),
        P(None, "ka", "pa"),
    )
    return jax.shard_map(
        functools.partial(on_device, mesh.shape["ka"], mesh.shape["pa"]),
        mesh=mesh,
        in_specs=placed,
        out_specs=(P("ka", None, "pa"), P("ka", None, "pa")),
        check_vma=False,
    )
```

```python
import functools
import math

import jax
import jax.numpy as jnp
from jax import lax
from jax.experimental import pallas as pl
from jax.experimental.pallas import tpu as pltpu
from jax.sharding import PartitionSpec as P

KY = 16
MESH = pl.DeviceIdType.MESH
LAG_NEXT = 2
LAG_PAIRS = 4
AHEAD = 3
GROUP = 1


def plus(a, b, sign=1.0):
    re = a[0] + b[0] if sign > 0 else a[0] - b[0]
    if b[1] is None:
        return (re, a[1])
    if a[1] is None:
        return (re, b[1] if sign > 0 else -b[1])
    return (re, a[1] + b[1] if sign > 0 else a[1] - b[1])


def conj(a):
    return a if a[1] is None else (a[0], -a[1])


def turn(a, step, size, sign):
    eighth = 8 * step // size if 8 * step % size == 0 else None
    if eighth == 0:
        return a
    if eighth == 2:
        re = None if a[1] is None else (-a[1] if sign > 0 else a[1])
        im = a[0] if sign > 0 else -a[0]
        return (jnp.zeros_like(im) if re is None else re, im)
    c = math.cos(2.0 * math.pi * step / size)
    s = sign * math.sin(2.0 * math.pi * step / size)
    if a[1] is None:
        return (c * a[0], s * a[0])
    if eighth == 1:
        return (c * (a[0] - sign * a[1]), c * (a[1] + sign * a[0]))
    if eighth == 3:
        return (c * (a[0] + sign * a[1]), c * (a[1] - sign * a[0]))
    return (c * a[0] - s * a[1], c * a[1] + s * a[0])


def complex_transform(x, sign):
    size = len(x)
    if size == 1:
        return x
    even = complex_transform(x[0::2], sign)
    odd = complex_transform(x[1::2], sign)
    odd = [turn(o, j, size, sign) for j, o in enumerate(odd)]
    first = [plus(e, o) for e, o in zip(even, odd)]
    return first + [plus(e, o, -1.0) for e, o in zip(even, odd)]


def real_forward(x):
    size = len(x)
    if size == 1:
        return [(x[0], None)]
    even, odd = real_forward(x[0::2]), real_forward(x[1::2])
    if size == 2:
        return [plus(even[0], odd[0]), plus(even[0], odd[0], -1.0)]
    out = [None] * (size // 2 + 1)
    for j in range(size // 4):
        t = turn(odd[j], j, size, -1)
        out[j] = plus(even[j], t)
        out[size // 2 - j] = conj(plus(even[j], t, -1.0))
    out[size // 4] = (even[size // 4][0], -odd[size // 4][0])
    return out


def real_backward(spectrum):
    size = 2 * (len(spectrum) - 1)
    if size == 2:
        a, b = spectrum[0][0], spectrum[1][0]
        return [a + b, a - b]
    even, odd = [], []
    for j in range(size // 4):
        mirrored = conj(spectrum[size // 2 - j])
        even.append(plus(spectrum[j], mirrored))
        odd.append(turn(plus(spectrum[j], mirrored, -1.0), j, size, 1))
    middle = spectrum[size // 4]
    even.append((2.0 * middle[0], None))
    odd.append((-2.0 * middle[1], None))
    out = [None] * size
    out[0::2] = real_backward(even)
    out[1::2] = real_backward(odd)
    return out


def screen_in_place(ref, weights):
    total, rows = ref.shape[0], ref.shape[1]
    wide = total // KY
    half = KY // 2
    scale = 0.5 / total
    assert rows % 8 == 0

    def fine_forward(i, carry):
        base, at = (i % wide) * KY, pl.ds(pl.multiple_of((i // wide) * 8, 8), 8)
        out = real_forward([ref[base + j, at, :] for j in range(KY)])
        for j in range(half + 1):
            ref[base + j, at, :] = out[j][0]
            if 0 < j < half:
                ref[base + KY - j, at, :] = out[j][1]
        return carry

    def fine_backward(i, carry):
        base, at = (i % wide) * KY, pl.ds(pl.multiple_of((i // wide) * 8, 8), 8)
        values = [ref[base + j, at, :] for j in range(KY)]
        spectrum = [(values[0], None)]
        spectrum += [(values[j], values[KY - j]) for j in range(1, half)]
        spectrum += [(values[half], None)]
        for j, value in enumerate(real_backward(spectrum)):
            ref[base + j, at, :] = value
        return carry

    def weight(q, finer, mirror, at):
        a = weights[q * KY + finer, at, :]
        b = weights[((wide - q) % wide) * KY + mirror, at, :]
        return (a + b) * scale

    def coarse_real(i, carry):
        at = pl.ds(pl.multiple_of(i * 8, 8), 8)
        for finer in (0, half):
            out = real_forward([ref[j * KY + finer, at, :] for j in range(wide)])
            scaled = []
            for q, (re, im) in enumerate(out):
                w = weight(q, finer, finer, at)
                scaled.append((re * w, None if im is None else im * w))
            for j, value in enumerate(real_backward(scaled)):
                ref[j * KY + finer, at, :] = value
        return carry

    def coarse_complex(i, carry):
        finer = 1 + i % (half - 1)
        mirror = KY - finer
        at = pl.ds(pl.multiple_of((i // (half - 1)) * 8, 8), 8)
        x = [(ref[j * KY + finer, at, :], ref[j * KY + mirror, at, :]) for j in range(wide)]
        scaled = []
        for q, (re, im) in enumerate(complex_transform(x, -1)):
            w = weight(q, finer, mirror, at)
            scaled.append((re * w, im * w))
        for j, (re, im) in enumerate(complex_transform(scaled, 1)):
            ref[j * KY + finer, at, :] = re
            ref[j * KY + mirror, at, :] = im
        return carry

    blocks = rows // 8
    lax.fori_loop(0, blocks * wide, fine_forward, 0)
    lax.fori_loop(0, blocks, coarse_real, 0)
    lax.fori_loop(0, blocks * (half - 1), coarse_complex, 0)
    lax.fori_loop(0, blocks * wide, fine_backward, 0)


def split(a):
    high = a.astype(jnp.bfloat16)
    return high, (a - high.astype(jnp.float32)).astype(jnp.bfloat16)


def product(a, b, left, right):
    (ah, al), (bh, bl) = a, b
    return lax.dot_general(
        jnp.concatenate([ah, ah, al], axis=left),
        jnp.concatenate([bh, bl, bh], axis=right),
        dimension_numbers=(((left,), (right,)), ((), ())),
        preferred_element_type=jnp.float32,
    )


def fused_kernel(
    ka, previous_in, current_in, energies_in, valence_in, conduction_in, weights_in,
    next_one, next_two, previous, current, energies, valence, conduction, weights,
    other_x, pairs, owned, returned, sent_sum, other_sum, own_sum,
    turned_parts, valence_parts, conduction_parts,
    load_sem, x_send, x_recv, pair_send, pair_recv, back_send, back_recv, sum_send, sum_recv,
):
    me, mine = lax.axis_index("ka"), lax.axis_index("pa")
    other = 1 - mine
    count, _, width = current.shape
    rows = weights.shape[1]
    own_c = pl.ds(pl.multiple_of(mine * width, width), width)
    other_c = pl.ds(pl.multiple_of(other * width, width), width)
    own_rows = pl.ds(pl.multiple_of(me * rows, rows), rows)

    def load(i):
        pairs_of = (
            (conduction_in, conduction), (valence_in, valence), (current_in, current),
            (weights_in, weights), (energies_in, energies), (previous_in, previous),
        )
        return pltpu.make_async_copy(pairs_of[i][0], pairs_of[i][1], load_sem.at[i])

    for i in range(6):
        load(i).start()
    barrier = pltpu.get_barrier_semaphore()

    def greet(j, carry):
        pl.semaphore_signal(
            barrier, inc=1, device_id={"ka": lax.rem(me + j, ka)}, device_id_type=MESH
        )
        return carry

    lax.fori_loop(1, ka, greet, 0)
    pl.semaphore_signal(barrier, inc=1, device_id={"pa": other}, device_id_type=MESH)
    pl.semaphore_wait(barrier, ka)

    def x_copy(turn_, k):
        source = (current_in, next_one)[turn_]
        return pltpu.make_async_remote_copy(
            src_ref=source.at[k], dst_ref=other_x.at[turn_, k],
            send_sem=x_send.at[turn_, k], recv_sem=x_recv.at[turn_, k],
            device_id={"pa": other}, device_id_type=MESH,
        )

    def sum_copy(turn_, k):
        return pltpu.make_async_remote_copy(
            src_ref=sent_sum.at[turn_, k], dst_ref=other_sum.at[turn_, k],
            send_sem=sum_send.at[turn_, k], recv_sem=sum_recv.at[turn_, k],
            device_id={"pa": other}, device_id_type=MESH,
        )

    def prepare(k, carry):
        rows_of = jnp.concatenate([conduction[k, own_c, :], conduction[k, other_c, :]], axis=0)
        conduction_parts[0, k], conduction_parts[1, k] = split(rows_of)
        valence_parts[0, k], valence_parts[1, k] = split(valence[k])
        turned_parts[0, k], turned_parts[1, k] = split(valence[k].T)
        return carry

    def parts(ref, k):
        return ref[0, k], ref[1, k]

    def pair_step(turn_, k):
        source = (current, next_one)[turn_]
        x_copy(turn_, k).wait_recv()
        if turn_ == 0:
            @pl.when(k + AHEAD < count)
            def _():
                x_copy(0, k + AHEAD).start()
        x = jnp.concatenate([source[k], other_x[turn_, k]], axis=1)
        inner = product(split(x), parts(conduction_parts, k), 1, 0)
        pairs[turn_, k] = product(parts(turned_parts, k), split(inner), 1, 0)

        owned[turn_, me * count + k] = pairs[turn_, k, own_rows, :]

        @pl.when(k % GROUP == GROUP - 1)
        def _():
            start = k - (GROUP - 1)
            for j in range(1, ka):
                peer = lax.rem(me + j, ka)
                mark = pl.ds(pl.multiple_of(peer * rows, rows), rows)
                pltpu.make_async_remote_copy(
                    src_ref=pairs.at[turn_, pl.ds(start, GROUP), mark],
                    dst_ref=owned.at[turn_, pl.ds(me * count + start, GROUP)],
                    send_sem=pair_send.at[turn_], recv_sem=pair_recv.at[turn_],
                    device_id={"ka": peer}, device_id_type=MESH,
                ).start()

    def wait_bytes(ref, sem):
        pltpu.make_async_copy(ref, ref, sem).wait()

    def send_back(turn_, g):
        for j in range(1, ka):
            peer = lax.rem(me + j, ka)
            pltpu.make_async_remote_copy(
                src_ref=owned.at[turn_, pl.ds(peer * count + g * GROUP, GROUP)],
                dst_ref=returned.at[turn_, pl.ds(g * GROUP, GROUP), own_rows],
                send_sem=back_send.at[turn_], recv_sem=back_recv.at[turn_, g],
                device_id={"ka": peer}, device_id_type=MESH,
            ).start()

    def screen(turn_):
        wait_bytes(owned.at[turn_, pl.ds(0, (ka - 1) * count)], pair_recv.at[turn_])
        screen_in_place(owned.at[turn_], weights)

        for g in range(min(AHEAD, count // GROUP)):
            send_back(turn_, g)

        def keep(k, carry):
            returned[turn_, k, own_rows, :] = owned[turn_, me * count + k]
            return carry

        lax.fori_loop(0, count, keep, 0)

    def sum_step(turn_, k):
        @pl.when(k % GROUP == 0)
        def _():
            g = k // GROUP
            group = pl.ds(k, GROUP)
            wait_bytes(returned.at[turn_, group, pl.ds(0, (ka - 1) * rows)], back_recv.at[turn_, g])

            @pl.when(g + AHEAD < count // GROUP)
            def _():
                send_back(turn_, g + AHEAD)

        partial_rows = product(split(returned[turn_, k]), parts(conduction_parts, k), 1, 1)
        term = product(parts(valence_parts, k), split(partial_rows), 1, 0)
        sent_sum[turn_, k] = term[:, width:]
        sum_copy(turn_, k).start()
        own_sum[k] = term[:, :width]

    def next_step(turn_, k):
        sum_copy(turn_, k).wait_recv()
        summed = own_sum[k] + other_sum[turn_, k]
        if turn_ == 0:
            next_one[k] = 2.0 * (energies[k] * current[k] + summed) - previous[k]
            x_copy(1, k).start()
        else:
            next_two[k] = 2.0 * (energies[k] * next_one[k] + summed) - current[k]

    def start_x(k, carry):
        x_copy(0, k).start()
        return carry

    lax.fori_loop(0, min(AHEAD, count), start_x, 0)
    load(0).wait()
    load(1).wait()
    lax.fori_loop(0, count, prepare, 0)
    load(2).wait()

    def first_pairs(k, carry):
        pair_step(0, k)
        return carry

    lax.fori_loop(0, count, first_pairs, 0)
    for i in (3, 4, 5):
        load(i).wait()
    screen(0)

    def middle(t, carry):
        @pl.when(t < count)
        def _():
            sum_step(0, t)

        @pl.when(jnp.logical_and(t >= LAG_NEXT, t < count + LAG_NEXT))
        def _():
            next_step(0, t - LAG_NEXT)

        @pl.when(t >= LAG_PAIRS)
        def _():
            pair_step(1, t - LAG_PAIRS)

        return carry

    lax.fori_loop(0, count + LAG_PAIRS, middle, 0)
    screen(1)

    def last(t, carry):
        @pl.when(t < count)
        def _():
            sum_step(1, t)

        @pl.when(t >= LAG_NEXT)
        def _():
            next_step(1, t - LAG_NEXT)

        return carry

    lax.fori_loop(0, count + LAG_NEXT, last, 0)

    for turn_ in (0, 1):
        def sent(k, carry):
            x_copy(turn_, k).wait_send()
            sum_copy(turn_, k).wait_send()
            return carry

        lax.fori_loop(0, count, sent, 0)
        everything = owned.at[turn_, pl.ds(0, (ka - 1) * count)]
        wait_bytes(everything, pair_send.at[turn_])
        wait_bytes(everything, back_send.at[turn_])


def fused(ka, previous, current, energies, valence, conduction, kernel):
    arrays = (previous, current, energies, valence, conduction, kernel)
    block, owned = current.shape, kernel.shape
    whole = pl.BlockSpec(memory_space=pltpu.VMEM)
    points = (block[0], valence.shape[2], kernel.shape[2])
    twice = lambda shape: pltpu.VMEM((2,) + shape, jnp.float32)
    halves = lambda *shape: pltpu.VMEM((2,) + shape, jnp.bfloat16)
    dma = pltpu.SemaphoreType.DMA
    return pl.pallas_call(
        functools.partial(fused_kernel, ka),
        out_shape=(jax.ShapeDtypeStruct(block, jnp.float32),) * 2,
        in_specs=[pl.BlockSpec(memory_space=pl.ANY)] * 6,
        out_specs=(whole, whole),
        scratch_shapes=[
            *(pltpu.VMEM(a.shape, jnp.float32) for a in arrays),
            twice(block), twice(points), twice(owned), twice(points),
            twice(block), twice(block), pltpu.VMEM(block, jnp.float32),
            halves(points[0], points[1], valence.shape[1]), halves(*valence.shape),
            halves(*conduction.shape),
            dma((6,)), dma((2, block[0])), dma((2, block[0])), dma((2,)), dma((2,)),
            dma((2,)), dma((2, block[0])), dma((2, block[0])), dma((2, block[0])),
        ],
        compiler_params=pltpu.CompilerParams(
            collective_id=0, has_side_effects=True, vmem_limit_bytes=52 * 2**20
        ),
    )(*arrays)


def phase_tables(total):
    points = jnp.arange(total)
    wide = total // KY
    coarse = points // KY
    finer = points % KY
    turns = (coarse[:, None] * coarse[None, :] % wide).astype(jnp.float32) / wide
    turns = turns + (finer[:, None] * finer[None, :] % KY).astype(jnp.float32) / KY
    angles = 2.0 * math.pi * turns
    return (jnp.cos(angles), jnp.sin(angles))


def screen_owned(flattened, kernel, cosine_table, sine_table):
    highest = lax.Precision.HIGHEST
    total = kernel.shape[0]
    even = jnp.dot(cosine_table, flattened, precision=highest)
    odd = jnp.dot(sine_table, flattened, precision=highest)
    weights = kernel.reshape(total, kernel.shape[1] * kernel.shape[2])
    return (
        jnp.dot(cosine_table, weights * even, precision=highest)
        + jnp.dot(sine_table, weights * odd, precision=highest)
    ) / total


def kernel_product(field, valence, conduction, kernel, cosine_table, sine_table):
    highest = lax.Precision.HIGHEST
    total = kernel.shape[0]
    inner = jnp.einsum("kvc,kcn->kvn", field, conduction, precision=highest)
    pair_blocks = jnp.einsum("kvm,kvn->kmn", valence, inner, precision=highest)
    owned = lax.all_to_all(pair_blocks, "ka", split_axis=1, concat_axis=0, tiled=True)
    flattened = owned.reshape(total, owned.shape[1] * owned.shape[2])
    screened = screen_owned(flattened, kernel, cosine_table, sine_table).reshape(owned.shape)
    returned = lax.all_to_all(screened, "ka", split_axis=0, concat_axis=1, tiled=True)
    partial_rows = jnp.einsum("kmn,kcn->kmc", returned, conduction, precision=highest)
    return jnp.einsum("kvm,kmc->kvc", valence, partial_rows, precision=highest)


def fits(ka, pa, current, conduction, kernel):
    wide = kernel.shape[0] // KY
    return (
        pa == 2
        and current.shape[2] == kernel.shape[2]
        and current.shape[2] % 128 == 0
        and kernel.shape[1] % 8 == 0
        and current.shape[0] % GROUP == 0
        and wide >= 2
        and wide & (wide - 1) == 0
    )


def on_device(ka, pa, previous, current, energies, valence, conduction, kernel):
    if fits(ka, pa, current, conduction, kernel):
        return fused(ka, previous, current, energies, valence, conduction, kernel)
    cosine_table, sine_table = phase_tables(kernel.shape[0])
    whole_current = lax.all_gather(current, "pa", axis=2, tiled=True)
    folded_term = kernel_product(
        whole_current, valence, conduction, kernel, cosine_table, sine_table
    )
    summed = lax.psum_scatter(folded_term, "pa", scatter_dimension=2, tiled=True)
    next_one = 2.0 * (energies * current + summed) - previous
    whole_next = lax.all_gather(next_one, "pa", axis=2, tiled=True)
    second_term = kernel_product(whole_next, valence, conduction, kernel, cosine_table, sine_table)
    second_sum = lax.psum_scatter(second_term, "pa", scatter_dimension=2, tiled=True)
    next_two = 2.0 * (energies * next_one + second_sum) - current
    return (next_one, next_two)


def solution(mesh):
    placed = (
        P("ka", None, "pa"),
        P("ka", None, "pa"),
        P("ka", None, "pa"),
        P("ka", None, None),
        P("ka", None, "pa"),
        P(None, "ka", "pa"),
    )
    return jax.shard_map(
        functools.partial(on_device, mesh.shape["ka"], mesh.shape["pa"]),
        mesh=mesh,
        in_specs=placed,
        out_specs=(P("ka", None, "pa"), P("ka", None, "pa")),
        check_vma=False,
    )
```
